1024 devices in a mesh: inner: 16 (over z), outer: 16 (over y, core), tensor: 4 (over x).
Axes of the slice: x: 4, y: 8, z: 16, core: 2. Of those that a mesh axis runs over, the one named last changes fastest.
Arguments:
- activations: bfloat16 [98304, 14848], P(('inner', 'outer'), 'tensor'), may hold values from -6 to 6
- out_grad: bfloat16 [98304, 1024], P(('inner', 'outer', 'tensor')), may hold values from -0.078125 to 0.078125
Outputs:
- weight_grad: float32 [1024, 14848], P(('inner', 'outer'), 'tensor')
The draws below stay inside these ranges and needn't reach their ends.
All inputs are finite; a program needn't handle non-finite values.
Results may differ from the reference program's by a relative error of at most 0.012.
Values may be sent and summed in bfloat16 or wider, within the bound.
No kernel may reach another device: no remote copies, remote signals or barrier semaphores. Data moves between devices by JAX's collectives and lax.ppermute only.
A program may use at most 32 MiB of HBM per device.

```python
import jax
import jax.numpy as jnp
from jax import lax

D_IN = 14848
TOK_DEV = 384
COLS = 1024
TOKENS = 98304
N_INNER = 16
N_OUTER = 16


def raised(result, key, source, target, parts, factor):
    owner, partner = [(jnp.arange(result.shape[position]) // (result.shape[position] // parts)).reshape([-1 if axis == position else 1 for axis in range(result.ndim)]) for position in (source, target)]
    chosen = jax.random.permutation(key, parts)[partner]
    strong = (owner == chosen) | (owner == (partner + parts // 2) % parts)
    return jnp.where(strong, factor * result, result)


def shard_levels(key, shape, pieces, least, high):
    level, own = 1.0, jax.random.fold_in(key, 6)
    for dim, parts in pieces:
        heights = jnp.exp(jax.random.uniform(jax.random.fold_in(own, dim), (parts,), jnp.float32, least / len(pieces), high / len(pieces)))
        level = level * jnp.repeat(heights, shape[dim] // parts).reshape([-1 if axis == dim else 1 for axis in range(len(shape))])
    return level


def noise(own_key, extent, scale, limit, pieces=(), kind=jnp.bfloat16):
    array = scale * jax.random.normal(own_key, extent, jnp.float32)
    if pieces:
        array = array * shard_levels(own_key, extent, pieces, -0.22, 0.18)
    return jnp.clip(array, -limit, limit).astype(kind)


def noise_with(rng, extent, scale, limit, pieces, heavy, kind=jnp.bfloat16):
    result = scale * jax.random.normal(rng, extent, jnp.float32)
    if pieces:
        result = result * shard_levels(rng, extent, pieces, -0.22, 0.18)
    return jnp.clip(raised(result, jax.random.fold_in(rng, 3), *heavy), -limit, limit).astype(kind)


def setup_inputs(seed: int = 0) -> dict:
    seeds = jax.random.split(jax.random.key(seed), 3)
    return {
        "activations": noise(seeds[0], (TOKENS, D_IN), 1.0, 6.0, ((0, 256), (1, 4))),
        "out_grad": noise_with(seeds[1], (TOKENS, COLS), (1.0 / (TOK_DEV * N_INNER * N_OUTER) ** 0.5), 0.078125, ((0, 1024),), (0, 1, 1024, 6.0)),
    }


def reference(activations, out_grad):
    inputs = activations.reshape(N_INNER, N_OUTER, TOK_DEV, D_IN)
    grads = out_grad.reshape(N_INNER, N_OUTER, TOK_DEV, COLS)

    def outer_step(total, outer_index):
        def inner_step(acc, inner_index):
            part = jnp.dot(grads[inner_index, outer_index].T, inputs[inner_index, outer_index], preferred_element_type=jnp.float32)
            rounded = lax.optimization_barrier(part.astype(jnp.bfloat16))
            return acc + rounded.astype(jnp.float32), None

        acc, unused = lax.scan(inner_step, jnp.zeros((COLS, D_IN), jnp.float32), jnp.arange(N_INNER))
        level = lax.optimization_barrier(acc.astype(jnp.bfloat16))
        return total + level.astype(jnp.float32), None

    total, unused = lax.scan(outer_step, jnp.zeros((COLS, D_IN), jnp.float32), jnp.arange(N_OUTER))
    return total
```

```python
import jax
import jax.numpy as jnp
from jax import lax
from jax.sharding import PartitionSpec as P

LANES = 128


def on_device(activations, out_grad):
    width = activations.shape[1]
    columns = out_grad.shape[1]
    owners = lax.axis_size("inner") * lax.axis_size("outer")
    rows = columns // owners
    groups = width // LANES
    partial_sum = lax.dot_general(
        lax.all_gather(out_grad, "tensor", axis=0, tiled=True),
        activations,
        (((0,), (0,)), ((), ())),
        preferred_element_type=jnp.float32,
    ).astype(jnp.bfloat16)
    packed = partial_sum.reshape(owners, rows, groups, LANES).transpose(0, 2, 1, 3)
    packed = packed.reshape(owners, groups * rows, LANES)
    total = lax.psum_scatter(packed, ("inner", "outer"), scatter_dimension=0, tiled=True)
    total = total.reshape(groups, rows, LANES).transpose(1, 0, 2)
    return total.reshape(rows, width).astype(jnp.float32)


def solution(mesh):
    in_specs = (P(("inner", "outer"), "tensor"), P(("inner", "outer", "tensor"), None))
    out_specs = P(("inner", "outer"), "tensor")
    return jax.shard_map(
        on_device, mesh=mesh, in_specs=in_specs, out_specs=out_specs, check_vma=False
    )
```

```python
import jax
import jax.numpy as jnp
from jax import lax
from jax.sharding import Mesh, PartitionSpec as P

LANES = 128


def pairs(count):
    return [(i, i ^ 1) for i in range(count)]


def on_device(activations, out_grad):
    tokens, width = activations.shape
    core = lax.axis_index("core")
    first = core == 0
    half = -(-(width // LANES) // 2) * LANES
    low, high = activations[:, :half], activations[:, width - half :]
    received = lax.ppermute(jnp.where(first, high, low), "core", pairs(2))
    kept = jnp.where(first, low, high)
    grads = lax.all_gather(out_grad, "x", axis=0, tiled=True)
    grads_other = lax.ppermute(grads, "core", pairs(2))
    contract = (((0,), (0,)), ((), ()))
    partial_sum = lax.dot_general(
        jnp.concatenate([grads, grads_other], axis=0),
        jnp.concatenate([kept, received], axis=0),
        contract,
        preferred_element_type=jnp.float32,
    ).astype(jnp.bfloat16)
    over_inner = lax.psum_scatter(partial_sum, "inner", scatter_dimension=0, tiled=True)
    count = lax.axis_size("y")
    rows = over_inner.shape[0] // count
    blocks = lax.all_to_all(
        over_inner.reshape(count, rows, half), "y", split_axis=0, concat_axis=0, tiled=True
    )
    total = jnp.sum(blocks, axis=0, dtype=jnp.float32)
    mine = rows // 2
    top, bottom = total[:mine], total[mine:]
    own = jnp.where(first, top, bottom)
    other = lax.ppermute(jnp.where(first, bottom, top), "core", pairs(2))
    overlap = 2 * half - width
    left = jnp.where(first, own, other)
    right = jnp.where(first, other, own)
    return jnp.concatenate([left, right[:, overlap:]], axis=1)


def solution(mesh):
    inner, outer, tensor = (mesh.shape[name] for name in ("inner", "outer", "tensor"))
    fine = Mesh(
        mesh.devices.reshape(inner, outer // 2, 2, tensor), ("inner", "y", "core", "x")
    )
    in_specs = (P(("inner", "y", "core"), "x"), P(("inner", "y", "core", "x"), None))
    out_specs = P(("inner", "y", "core"), "x")
    return jax.shard_map(
        on_device, mesh=fine, in_specs=in_specs, out_specs=out_specs, check_vma=False
    )
```

```python
import jax
import jax.numpy as jnp
from jax import lax
from jax.sharding import Mesh, PartitionSpec as P

LANES = 128
SWAP = [(0, 1), (1, 0)]


def in_owner_order(out_grad, inner, outer):
    columns = out_grad.shape[1]
    rows = columns // (inner * outer * 2)
    new = lax.broadcasted_iota(jnp.int32, (columns, columns), 1)
    old = lax.broadcasted_iota(jnp.int32, (columns, columns), 0)
    row, rest = new % rows, new // rows
    i, rest = rest % inner, rest // inner
    y, core = rest % outer, rest // outer
    source = ((i * outer + y) * 2 + core) * rows + row
    one_hot = (source == old).astype(out_grad.dtype)
    moved = lax.dot_general(
        out_grad, one_hot, (((1,), (0,)), ((), ())), preferred_element_type=jnp.float32
    )
    return moved.astype(out_grad.dtype)


def add(left, right):
    return (left.astype(jnp.float32) + right.astype(jnp.float32)).astype(jnp.bfloat16)


def on_device(activations, out_grad):
    inner, outer = lax.axis_size("inner"), lax.axis_size("y")
    core, me = lax.axis_index("core"), lax.axis_index("y")
    width = activations.shape[1]
    activations_other = lax.ppermute(activations, "core", SWAP)
    grads = lax.all_gather(in_owner_order(out_grad, inner, outer), "x", axis=0, tiled=True)
    columns = grads.shape[1] // 2
    grads_own = lax.dynamic_slice_in_dim(grads, core * columns, columns, 1, allow_negative_indices=False)
    grads_sent = lax.dynamic_slice_in_dim(
        grads, (1 - core) * columns, columns, 1, allow_negative_indices=False
    )
    grads_other = lax.ppermute(grads_sent, "core", SWAP)
    all_grads = jnp.concatenate([grads_own, grads_other], axis=0)
    cut = -(-(width // LANES) // 2) * LANES

    def partial_sum(low, high):
        tokens = jnp.concatenate([activations[:, low:high], activations_other[:, low:high]], axis=0)
        product = lax.dot_general(
            all_grads, tokens, (((0,), (0,)), ((), ())), preferred_element_type=jnp.float32
        )
        return product.astype(jnp.bfloat16).reshape(outer, columns // outer, high - low)

    pieces = (partial_sum(0, cut), partial_sum(cut, width))

    def of(piece, distance):
        owner = lax.rem(me + (distance + outer), outer)
        return lax.dynamic_index_in_dim(piece, owner, 0, keepdims=False, allow_negative_indices=False)

    far = outer // 2
    streams = [(p, sign, far if (sign > 0) == (p == 0) else far - 1) for sign in (1, -1) for p in (0, 1)]
    moving = {}
    for distance in range(far, 0, -1):
        for p, sign, hops in streams:
            if distance > hops:
                continue
            own = of(pieces[p], sign * distance)
            block = own if distance == hops else add(moving[p, sign], own)
            moving[p, sign] = lax.ppermute(
                block, "y", [(s, (s + sign) % outer) for s in range(outer)]
            )
    sums = [
        (
            of(pieces[p], 0).astype(jnp.float32)
            + moving[p, 1].astype(jnp.float32)
            + moving[p, -1].astype(jnp.float32)
        ).astype(jnp.bfloat16)
        for p in (0, 1)
    ]
    first = jnp.concatenate(sums, axis=1).reshape(inner, columns // outer // inner, width)
    blocks = lax.all_to_all(first, "inner", split_axis=0, concat_axis=0, tiled=True)
    return jnp.sum(blocks, axis=0, dtype=jnp.float32)


def solution(mesh):
    inner, outer, tensor = (mesh.shape[name] for name in ("inner", "outer", "tensor"))
    fine = Mesh(
        mesh.devices.reshape(inner, outer // 2, 2, tensor), ("inner", "y", "core", "x")
    )
    in_specs = (P(("inner", "y", "core"), "x"), P(("inner", "y", "core", "x"), None))
    out_specs = P(("inner", "y", "core"), "x")
    return jax.shard_map(
        on_device, mesh=fine, in_specs=in_specs, out_specs=out_specs, check_vma=False
    )
```

```python
import jax
import jax.numpy as jnp
from jax import lax
from jax.sharding import Mesh, PartitionSpec as P

LANES = 128
SWAP = [(0, 1), (1, 0)]


def in_owner_order(out_grad, inner, outer):
    columns = out_grad.shape[1]
    rows = columns // (inner * outer * 2)
    new = lax.broadcasted_iota(jnp.int32, (columns, columns), 1)
    old = lax.broadcasted_iota(jnp.int32, (columns, columns), 0)
    row, rest = new % rows, new // rows
    i, rest = rest % inner, rest // inner
    y, core = rest % outer, rest // outer
    source = ((i * outer + y) * 2 + core) * rows + row
    one_hot = (source == old).astype(out_grad.dtype)
    moved = lax.dot_general(
        out_grad, one_hot, (((1,), (0,)), ((), ())), preferred_element_type=jnp.float32
    )
    return moved.astype(out_grad.dtype)


def add(left, right):
    return (left.astype(jnp.float32) + right.astype(jnp.float32)).astype(jnp.bfloat16)


def on_device(activations, out_grad):
    inner, outer = lax.axis_size("inner"), lax.axis_size("y")
    core, me = lax.axis_index("core"), lax.axis_index("y")
    width = activations.shape[1]
    ordered = in_owner_order(out_grad, inner, outer)
    columns = ordered.shape[1] // 2

    def half_of(owner):
        return lax.dynamic_slice_in_dim(
            ordered, owner * columns, columns, 1, allow_negative_indices=False
        )

    grads_other = lax.ppermute(half_of(1 - core), "core", SWAP)
    grads_other, sent = lax.optimization_barrier((grads_other, activations))
    activations_other = lax.ppermute(sent, "core", SWAP)
    grads = jnp.stack([half_of(core), grads_other])
    grads = lax.all_gather(grads, "x", axis=1, tiled=True)
    tokens = jnp.concatenate([activations, activations_other], axis=0)
    chunks = lax.dot_general(
        grads.reshape(tokens.shape[0], columns),
        tokens,
        (((0,), (0,)), ((), ())),
        preferred_element_type=jnp.float32,
    ).astype(jnp.bfloat16).reshape(outer, columns // outer, width)
    cut = -(-(width // LANES) // 2) * LANES
    spans = ((0, cut), (cut, width - cut))

    pairings = (
        [(s, s ^ 1) for s in range(outer)],
        [((s + 1) % outer, ((s ^ 1) + 1) % outer) for s in range(outer)],
    )
    way = 1 - 2 * lax.rem(me, 2)

    def own(piece, pairing, distance):
        start, size = spans[piece]
        owner = lax.rem(me + way * (distance if pairing == 0 else -distance) + outer, outer)
        block = lax.dynamic_slice(
            chunks, (owner, 0, start), (1, chunks.shape[1], size), allow_negative_indices=False
        )
        return block[0]

    far = outer // 2
    arrived = {}
    for distance in range(far, 0, -1):
        leaving = {}
        for piece in (0, 1):
            for pairing in (0, 1):
                if distance == far and piece != pairing:
                    continue
                block = own(piece, pairing, distance)
                if (piece, 1 - pairing) in arrived:
                    block = add(arrived[piece, 1 - pairing], block)
                elif (piece, pairing) in arrived:
                    block, arrived[piece, pairing] = lax.optimization_barrier(
                        (block, arrived[piece, pairing])
                    )
                leaving[piece, pairing] = lax.ppermute(block, "y", pairings[pairing])
        arrived = leaving
    sums = [
        (
            own(piece, 0, 0).astype(jnp.float32)
            + arrived[piece, 0].astype(jnp.float32)
            + arrived[piece, 1].astype(jnp.float32)
        ).astype(jnp.bfloat16)
        for piece in (0, 1)
    ]
    first = jnp.concatenate(sums, axis=1).reshape(inner, columns // outer // inner, width)
    blocks = lax.all_to_all(first, "inner", split_axis=0, concat_axis=0, tiled=True)
    return jnp.sum(blocks, axis=0, dtype=jnp.float32)


def solution(mesh):
    inner, outer, tensor = (mesh.shape[name] for name in ("inner", "outer", "tensor"))
    fine = Mesh(
        mesh.devices.reshape(inner, outer // 2, 2, tensor), ("inner", "y", "core", "x")
    )
    in_specs = (P(("inner", "y", "core"), "x"), P(("inner", "y", "core", "x"), None))
    out_specs = P(("inner", "y", "core"), "x")
    return jax.shard_map(
        on_device, mesh=fine, in_specs=in_specs, out_specs=out_specs, check_vma=False
    )
```

```python
import jax
import jax.numpy as jnp
from jax import lax
from jax.sharding import Mesh, PartitionSpec as P

LANES = 128
SWAP = [(0, 1), (1, 0)]


def in_owner_order(out_grad, far, near, outer):
    columns = out_grad.shape[1]
    rows = columns // (far * near * outer * 2)
    new = lax.broadcasted_iota(jnp.int32, (columns, columns), 1)
    old = lax.broadcasted_iota(jnp.int32, (columns, columns), 0)
    row, rest = new % rows, new // rows
    f, rest = rest % far, rest // far
    y, rest = rest % outer, rest // outer
    n, core = rest % near, rest // near
    source = (((f * near + n) * outer + y) * 2 + core) * rows + row
    one_hot = (source == old).astype(out_grad.dtype)
    moved = lax.dot_general(
        out_grad, one_hot, (((1,), (0,)), ((), ())), preferred_element_type=jnp.float32
    )
    return moved.astype(out_grad.dtype)


def pairings_of(count):
    return (
        [(s, s ^ 1) for s in range(count)],
        [((s + 1) % count, ((s ^ 1) + 1) % count) for s in range(count)],
    )


def on_device(activations, out_grad):
    far_z, near_z, outer = (lax.axis_size(name) for name in ("far", "near", "y"))
    core, me, near = (lax.axis_index(name) for name in ("core", "y", "near"))
    width = activations.shape[1]
    ordered = in_owner_order(out_grad, far_z, near_z, outer)
    columns = ordered.shape[1] // 2

    def half_of(owner):
        return lax.dynamic_slice_in_dim(
            ordered, owner * columns, columns, 1, allow_negative_indices=False
        )

    grads_other = lax.ppermute(half_of(1 - core), "core", SWAP)
    grads_other, sent = lax.optimization_barrier((grads_other, activations))
    activations_other = lax.ppermute(sent, "core", SWAP)
    grads = jnp.stack([half_of(core), grads_other])
    grads = lax.all_gather(grads, "x", axis=1, tiled=True)
    grads = grads.reshape(2 * grads.shape[1], columns)
    rows = columns // outer // near_z
    half = columns // near_z

    def rows_for(owner, mine, theirs):
        product = lax.dot_general(
            lax.dynamic_slice_in_dim(grads, owner * half, half, 1, allow_negative_indices=False),
            jnp.concatenate([mine, theirs], axis=0),
            (((0,), (0,)), ((), ())),
            preferred_element_type=jnp.float32,
        )
        return product.astype(jnp.bfloat16).reshape(outer, rows, width)

    leaving = rows_for(1 - near, activations, activations_other)
    kept = rows_for(near, *lax.optimization_barrier((activations, activations_other)))

    groups = width // LANES
    part = groups * 5 // 18
    cut, middle = (LANES * (groups - 2 * part), LANES * (groups - part))
    pieces = (((0, cut),), ((cut, middle), (middle, width)))

    def block_of(source, owner, low, high):
        block = lax.dynamic_slice(
            source, (owner, 0, low), (1, rows, high - low), allow_negative_indices=False
        )
        return block[0].astype(jnp.float32)

    z_pairings = pairings_of(far_z * near_z)
    incoming = [
        lax.ppermute(leaving[:, :, low:high], ("far", "near"), z_pairings[k])
        for k, (low, high) in enumerate(pieces[1])
    ]

    y_pairings = pairings_of(outer)
    way = 1 - 2 * lax.rem(me, 2)

    def own(piece, pairing, distance):
        owner = lax.rem(me + way * (distance if pairing == 0 else -distance) + outer, outer)
        if piece == 0:
            sources = (leaving, kept)
            return jnp.concatenate([block_of(rows_, owner, 0, cut) for rows_ in sources], axis=0)
        parts = [
            block_of(kept, owner, low, high) + block_of(incoming[k], owner, 0, high - low)
            for k, (low, high) in enumerate(pieces[1])
        ]
        return jnp.concatenate(parts, axis=1)

    farthest = outer // 2

    def step(piece, distance, arrived):
        blocks = {}
        for pairing in (0, 1):
            if distance == farthest and piece != pairing:
                continue
            block = own(piece, pairing, distance)
            if 1 - pairing in arrived:
                block = block + arrived[1 - pairing].astype(jnp.float32)
            blocks[pairing] = block.astype(jnp.bfloat16)
        if distance == farthest - 1:
            blocks = lax.optimization_barrier(blocks)
        moved = {k: lax.ppermute(block, "y", y_pairings[k]) for k, block in blocks.items()}
        return lax.optimization_barrier(moved)

    arrived = [{}, {}]
    for distance in range(farthest, 0, -1):
        for piece in (0, 1):
            arrived[piece] = step(piece, distance, arrived[piece])
            if distance == farthest and piece == 0:
                arrived[0], incoming[:] = lax.optimization_barrier((arrived[0], incoming))
    sums = [
        own(piece, 0, 0)
        + arrived[piece][0].astype(jnp.float32)
        + arrived[piece][1].astype(jnp.float32)
        for piece in (0, 1)
    ]
    late_other = lax.ppermute(sums[0][:rows].astype(jnp.bfloat16), "near", SWAP)
    late = sums[0][rows:] + late_other.astype(jnp.float32)
    first = jnp.concatenate([late.astype(jnp.bfloat16), sums[1].astype(jnp.bfloat16)], axis=1)
    first = first.reshape(far_z, rows // far_z, width)
    blocks = lax.all_to_all(first, "far", split_axis=0, concat_axis=0, tiled=True)
    return jnp.sum(blocks, axis=0, dtype=jnp.float32)


def solution(mesh):
    inner, outer, tensor = (mesh.shape[name] for name in ("inner", "outer", "tensor"))
    fine = Mesh(
        mesh.devices.reshape(inner // 2, 2, outer // 2, 2, tensor),
        ("far", "near", "y", "core", "x"),
    )
    groups = ("far", "near", "y", "core")
    in_specs = (P(groups, "x"), P(groups + ("x",), None))
    return jax.shard_map(
        on_device, mesh=fine, in_specs=in_specs, out_specs=P(groups, "x"), check_vma=False
    )
```

```python
import jax
import jax.numpy as jnp
from jax import lax
from jax.sharding import Mesh, PartitionSpec as P

LANES = 128
SWAP = [(0, 1), (1, 0)]


def in_owner_order(out_grad, inner, outer):
    columns = out_grad.shape[1]
    rows = columns // (inner * outer * 2)
    new = lax.broadcasted_iota(jnp.int32, (columns, columns), 1)
    old = lax.broadcasted_iota(jnp.int32, (columns, columns), 0)
    row, rest = new % rows, new // rows
    i, rest = rest % inner, rest // inner
    y, core = rest % outer, rest // outer
    source = ((i * outer + y) * 2 + core) * rows + row
    one_hot = (source == old).astype(out_grad.dtype)
    moved = lax.dot_general(
        out_grad, one_hot, (((1,), (0,)), ((), ())), preferred_element_type=jnp.float32
    )
    return moved.astype(out_grad.dtype)


def on_device(activations, out_grad):
    inner, outer = lax.axis_size("inner"), lax.axis_size("y")
    core, me = lax.axis_index("core"), lax.axis_index("y")
    width = activations.shape[1]
    ordered = in_owner_order(out_grad, inner, outer)
    columns = ordered.shape[1] // 2

    def half_of(owner):
        return lax.dynamic_slice_in_dim(
            ordered, owner * columns, columns, 1, allow_negative_indices=False
        )

    grads_other = lax.ppermute(half_of(1 - core), "core", SWAP)
    grads_other, sent = lax.optimization_barrier((grads_other, activations))
    activations_other = lax.ppermute(sent, "core", SWAP)
    grads = jnp.stack([half_of(core), grads_other])
    grads = lax.all_gather(grads, "x", axis=1, tiled=True)
    tokens = jnp.concatenate([activations, activations_other], axis=0)
    chunks = lax.dot_general(
        grads.reshape(tokens.shape[0], columns),
        tokens,
        (((0,), (0,)), ((), ())),
        preferred_element_type=jnp.float32,
    ).astype(jnp.bfloat16).reshape(outer, columns // outer, width)
    cut = -(-(width // LANES) // 2) * LANES

    pairings = (
        [s ^ 1 for s in range(outer)],
        [(((s + outer - 1) ^ 1) + 1) % outer for s in range(outer)],
    )
    swaps = [
        [(2 * s + c, 2 * pairings[(c + k) % 2][s] + c) for s in range(outer) for c in (0, 1)]
        for k in (0, 1)
    ]
    way = (1 - 2 * lax.rem(me, 2)) * (1 - 2 * core)

    def own(swap, distance, low=0, high=width):
        owner = lax.rem(me + way * (distance if swap == 0 else -distance) + outer, outer)
        block = lax.dynamic_slice(
            chunks, (owner, 0, low), (1, chunks.shape[1], high - low), allow_negative_indices=False
        )
        return block[0].astype(jnp.float32)

    farthest = outer // 2
    arrived, before = {}, None
    for distance in range(farthest, 0, -1):
        leaving = {}
        for swap in (0, 1) if (farthest - distance) % 2 == 0 else (1, 0):
            if distance == farthest:
                block = own(swap, distance, *((0, cut) if swap == 0 else (cut, width)))
            else:
                come, before = lax.optimization_barrier((arrived[1 - swap], before))
                come = come.astype(jnp.float32)
                if distance < farthest - 1:
                    block = own(swap, distance) + come
                else:
                    left, right = own(swap, distance, 0, cut), own(swap, distance, cut, width)
                    sides = (left + come, right) if swap == 1 else (left, right + come)
                    block = jnp.concatenate(sides, axis=1)
            before = block.astype(jnp.bfloat16)
            leaving[swap] = lax.ppermute(before, ("y", "core"), swaps[swap])
        arrived = leaving
    total = own(0, 0) + arrived[0].astype(jnp.float32) + arrived[1].astype(jnp.float32)
    first = total.astype(jnp.bfloat16).reshape(inner, columns // outer // inner, width)
    blocks = lax.all_to_all(first, "inner", split_axis=0, concat_axis=0, tiled=True)
    return jnp.sum(blocks, axis=0, dtype=jnp.float32)


def solution(mesh):
    inner, outer, tensor = (mesh.shape[name] for name in ("inner", "outer", "tensor"))
    fine = Mesh(
        mesh.devices.reshape(inner, outer // 2, 2, tensor), ("inner", "y", "core", "x")
    )
    in_specs = (P(("inner", "y", "core"), "x"), P(("inner", "y", "core", "x"), None))
    out_specs = P(("inner", "y", "core"), "x")
    return jax.shard_map(
        on_device, mesh=fine, in_specs=in_specs, out_specs=out_specs, check_vma=False
    )
```

```python
import jax
import jax.numpy as jnp
from jax import lax
from jax.sharding import Mesh, PartitionSpec as P

LANES = 128
SWAP = [(0, 1), (1, 0)]


def in_owner_order(out_grad, inner, outer):
    columns = out_grad.shape[1]
    rows = columns // (inner * outer * 2)
    new = lax.broadcasted_iota(jnp.int32, (columns, columns), 1)
    old = lax.broadcasted_iota(jnp.int32, (columns, columns), 0)
    row, rest = new % rows, new // rows
    i, rest = rest % inner, rest // inner
    y, core = rest % outer, rest // outer
    source = ((i * outer + y) * 2 + core) * rows + row
    one_hot = (source == old).astype(out_grad.dtype)
    moved = lax.dot_general(
        out_grad, one_hot, (((1,), (0,)), ((), ())), preferred_element_type=jnp.float32
    )
    return moved.astype(out_grad.dtype)


def on_device(activations, out_grad):
    inner, outer = lax.axis_size("inner"), lax.axis_size("y")
    core, me = lax.axis_index("core"), lax.axis_index("y")
    width = activations.shape[1]
    ordered = in_owner_order(out_grad, inner, outer)
    columns = ordered.shape[1] // 2

    def half_of(owner):
        return lax.dynamic_slice_in_dim(
            ordered, owner * columns, columns, 1, allow_negative_indices=False
        )

    grads_other = lax.ppermute(half_of(1 - core), "core", SWAP)
    grads_other, sent = lax.optimization_barrier((grads_other, activations))
    activations_other = lax.ppermute(sent, "core", SWAP)
    grads = jnp.stack([half_of(core), grads_other])
    grads = lax.all_gather(grads, "x", axis=1, tiled=True)
    tokens = jnp.concatenate([activations, activations_other], axis=0)
    chunks = lax.dot_general(
        grads.reshape(tokens.shape[0], columns),
        tokens,
        (((0,), (0,)), ((), ())),
        preferred_element_type=jnp.float32,
    ).astype(jnp.bfloat16).reshape(outer, columns // outer, width)
    cut = -(-(width // LANES) // 2) * LANES

    pairings = (
        [s ^ 1 for s in range(outer)],
        [(((s + outer - 1) ^ 1) + 1) % outer for s in range(outer)],
    )
    swaps = [
        [(2 * s + c, 2 * pairings[(c + k) % 2][s] + c) for s in range(outer) for c in (0, 1)]
        for k in (0, 1)
    ]
    way = (1 - 2 * lax.rem(me, 2)) * (1 - 2 * core)

    spans = ((0, cut), (cut, width))

    def own(piece, swap, distance):
        low, high = spans[piece]
        owner = lax.rem(me + way * (distance if swap == 0 else -distance) + outer, outer)
        block = lax.dynamic_slice(
            chunks, (owner, 0, low), (1, chunks.shape[1], high - low), allow_negative_indices=False
        )
        return block[0].astype(jnp.float32)

    farthest = outer // 2
    order = [(farthest, 0, 0), (farthest, 1, 1)]
    for distance in range(farthest - 1, 0, -1):
        first_way = (farthest - 1 - distance) % 2
        order += [(distance, p, p ^ first_way ^ late) for late in (0, 1) for p in (0, 1)]
    arrived, before = {}, None
    for distance, piece, swap in order:
        block = own(piece, swap, distance)
        source = (distance + 1, piece, 1 - swap)
        if source in arrived:
            come, before = lax.optimization_barrier((arrived[source], before))
            block = (block + come.astype(jnp.float32)).astype(jnp.bfloat16)
        else:
            block = block.astype(jnp.bfloat16)
            if before is not None:
                block, before = lax.optimization_barrier((block, before))
        before = block
        arrived[distance, piece, swap] = lax.ppermute(block, ("y", "core"), swaps[swap])
    sums = []
    for piece in (0, 1):
        come = (arrived[1, piece, 0], arrived[1, piece, 1])
        come, before = lax.optimization_barrier((come, before))
        total = own(piece, 0, 0) + come[0].astype(jnp.float32) + come[1].astype(jnp.float32)
        before = total.astype(jnp.bfloat16)
        sums.append(before)
    first = jnp.concatenate(sums, axis=1)
    first = first.reshape(inner, columns // outer // inner, width)
    blocks = lax.all_to_all(first, "inner", split_axis=0, concat_axis=0, tiled=True)
    return jnp.sum(blocks, axis=0, dtype=jnp.float32)


def solution(mesh):
    inner, outer, tensor = (mesh.shape[name] for name in ("inner", "outer", "tensor"))
    fine = Mesh(
        mesh.devices.reshape(inner, outer // 2, 2, tensor), ("inner", "y", "core", "x")
    )
    in_specs = (P(("inner", "y", "core"), "x"), P(("inner", "y", "core", "x"), None))
    out_specs = P(("inner", "y", "core"), "x")
    return jax.shard_map(
        on_device, mesh=fine, in_specs=in_specs, out_specs=out_specs, check_vma=False
    )
```

```python
import jax
import jax.numpy as jnp
from jax import lax
from jax.sharding import Mesh, PartitionSpec as P

LANES = 128
SWAP = [(0, 1), (1, 0)]


def in_owner_order(out_grad, inner, outer):
    columns = out_grad.shape[1]
    rows = columns // (inner * outer * 2)
    new = lax.broadcasted_iota(jnp.int32, (columns, columns), 1)
    old = lax.broadcasted_iota(jnp.int32, (columns, columns), 0)
    row, rest = new % rows, new // rows
    i, rest = rest % inner, rest // inner
    y, core = rest % outer, rest // outer
    source = ((i * outer + y) * 2 + core) * rows + row
    one_hot = (source == old).astype(out_grad.dtype)
    moved = lax.dot_general(
        out_grad, one_hot, (((1,), (0,)), ((), ())), preferred_element_type=jnp.float32
    )
    return moved.astype(out_grad.dtype)


def on_device(activations, out_grad):
    inner, outer = lax.axis_size("inner"), lax.axis_size("y")
    core, me = lax.axis_index("core"), lax.axis_index("y")
    width = activations.shape[1]
    ordered = in_owner_order(out_grad, inner, outer)
    columns = ordered.shape[1] // 2

    def half_of(owner):
        return lax.dynamic_slice_in_dim(
            ordered, owner * columns, columns, 1, allow_negative_indices=False
        )

    grads_other = lax.ppermute(half_of(1 - core), "core", SWAP)
    grads_other, sent = lax.optimization_barrier((grads_other, activations))
    activations_other = lax.ppermute(sent, "core", SWAP)
    grads = jnp.stack([half_of(core), grads_other])
    grads = lax.all_gather(grads, "x", axis=1, tiled=True)
    tokens = jnp.concatenate([activations, activations_other], axis=0)
    chunks = lax.dot_general(
        grads.reshape(tokens.shape[0], columns),
        tokens,
        (((0,), (0,)), ((), ())),
        preferred_element_type=jnp.float32,
    ).astype(jnp.bfloat16).reshape(outer, columns // outer, width)
    cut = -(-(width // LANES) // 2) * LANES

    pairings = (
        [s ^ 1 for s in range(outer)],
        [(((s + outer - 1) ^ 1) + 1) % outer for s in range(outer)],
    )
    swaps = [
        [(2 * s + c, 2 * pairings[(c + k) % 2][s] + c) for s in range(outer) for c in (0, 1)]
        for k in (0, 1)
    ]
    way = (1 - 2 * lax.rem(me, 2)) * (1 - 2 * core)

    spans = ((0, cut), (cut, width))

    def own(piece, swap, distance):
        low, high = spans[piece]
        owner = lax.rem(me + way * (distance if swap == 0 else -distance) + outer, outer)
        block = lax.dynamic_slice(
            chunks, (owner, 0, low), (1, chunks.shape[1], high - low), allow_negative_indices=False
        )
        return block[0].astype(jnp.float32)

    farthest = outer // 2
    order = [(farthest, 0, 0), (farthest, 1, 1)]
    for distance in range(farthest - 1, 0, -1):
        first_way = (farthest - 1 - distance) % 2
        order += [(distance, p, p ^ first_way ^ late) for late in (0, 1) for p in (0, 1)]
    arrived, before = {}, {}
    for distance, piece, swap in order:
        block = own(piece, swap, distance)
        source = (distance + 1, piece, 1 - swap)
        if source in arrived:
            come, before[piece] = lax.optimization_barrier((arrived[source], before[piece]))
            block = (block + come.astype(jnp.float32)).astype(jnp.bfloat16)
        else:
            block = block.astype(jnp.bfloat16)
        before[piece] = block
        arrived[distance, piece, swap] = lax.ppermute(block, ("y", "core"), swaps[swap])
    sums = []
    for piece in (0, 1):
        come = (arrived[1, piece, 0], arrived[1, piece, 1])
        total = own(piece, 0, 0) + come[0].astype(jnp.float32) + come[1].astype(jnp.float32)
        sums.append(total.astype(jnp.bfloat16))
    first = jnp.concatenate(sums, axis=1)
    first = first.reshape(inner, columns // outer // inner, width)
    blocks = lax.all_to_all(first, "inner", split_axis=0, concat_axis=0, tiled=True)
    return jnp.sum(blocks, axis=0, dtype=jnp.float32)


def solution(mesh):
    inner, outer, tensor = (mesh.shape[name] for name in ("inner", "outer", "tensor"))
    fine = Mesh(
        mesh.devices.reshape(inner, outer // 2, 2, tensor), ("inner", "y", "core", "x")
    )
    in_specs = (P(("inner", "y", "core"), "x"), P(("inner", "y", "core", "x"), None))
    out_specs = P(("inner", "y", "core"), "x")
    return jax.shard_map(
        on_device, mesh=fine, in_specs=in_specs, out_specs=out_specs, check_vma=False
    )
```

```python
import jax
import jax.numpy as jnp
from jax import lax
from jax.sharding import Mesh, PartitionSpec as P

LANES = 128
SWAP = [(0, 1), (1, 0)]


def in_owner_order(out_grad, inner, outer):
    columns = out_grad.shape[1]
    rows = columns // (inner * outer * 2)
    new = lax.broadcasted_iota(jnp.int32, (columns, columns), 1)
    old = lax.broadcasted_iota(jnp.int32, (columns, columns), 0)
    row, rest = new % rows, new // rows
    i, rest = rest % inner, rest // inner
    y, core = rest % outer, rest // outer
    source = ((i * outer + y) * 2 + core) * rows + row
    one_hot = (source == old).astype(out_grad.dtype)
    moved = lax.dot_general(
        out_grad, one_hot, (((1,), (0,)), ((), ())), preferred_element_type=jnp.float32
    )
    return moved.astype(out_grad.dtype)


def on_device(activations, out_grad):
    inner, outer = lax.axis_size("inner"), lax.axis_size("y")
    core, me = lax.axis_index("core"), lax.axis_index("y")
    width = activations.shape[1]
    ordered = in_owner_order(out_grad, inner, outer)
    columns = ordered.shape[1] // 2

    def half_of(owner):
        return lax.dynamic_slice_in_dim(
            ordered, owner * columns, columns, 1, allow_negative_indices=False
        )

    grads_other = lax.ppermute(half_of(1 - core), "core", SWAP)
    grads_other, sent = lax.optimization_barrier((grads_other, activations))
    activations_other = lax.ppermute(sent, "core", SWAP)
    grads = jnp.stack([half_of(core), grads_other])
    grads = lax.all_gather(grads, "x", axis=1, tiled=True)
    tokens = jnp.concatenate([activations, activations_other], axis=0)
    chunks = lax.dot_general(
        grads.reshape(tokens.shape[0], columns),
        tokens,
        (((0,), (0,)), ((), ())),
        preferred_element_type=jnp.float32,
    ).astype(jnp.bfloat16).reshape(outer, columns // outer, width)
    cut = -(-(width // LANES) // 2) * LANES

    pairings = (
        [s ^ 1 for s in range(outer)],
        [(((s + outer - 1) ^ 1) + 1) % outer for s in range(outer)],
    )
    swaps = [
        [(2 * s + c, 2 * pairings[(c + k) % 2][s] + c) for s in range(outer) for c in (0, 1)]
        for k in (0, 1)
    ]
    way = (1 - 2 * lax.rem(me, 2)) * (1 - 2 * core)

    spans = ((0, cut), (cut, width))

    def own(piece, swap, distance):
        low, high = spans[piece]
        owner = lax.rem(me + way * (distance if swap == 0 else -distance) + outer, outer)
        block = lax.dynamic_slice(
            chunks, (owner, 0, low), (1, chunks.shape[1], high - low), allow_negative_indices=False
        )
        return block[0].astype(jnp.float32)

    farthest = outer // 2
    order = [(farthest, 0, 0), (farthest, 1, 1)]
    for distance in range(farthest - 1, 0, -1):
        first_way = (farthest - 1 - distance) % 2
        order += [(distance, p, p ^ first_way ^ late) for late in (0, 1) for p in (0, 1)]
    arrived, before = {}, {}
    for distance, piece, swap in order:
        block = own(piece, swap, distance)
        source = (distance + 1, piece, 1 - swap)
        if source in arrived:
            come, before[piece] = lax.optimization_barrier((arrived[source], before[piece]))
            block = (block + come.astype(jnp.float32)).astype(jnp.bfloat16)
        else:
            block = block.astype(jnp.bfloat16)
            if piece in before:
                block, before[1 - piece] = lax.optimization_barrier((block, before[1 - piece]))
        before[piece] = block
        arrived[distance, piece, swap] = lax.ppermute(block, ("y", "core"), swaps[swap])
    sums = []
    for piece in (0, 1):
        come = (arrived[1, piece, 0], arrived[1, piece, 1])
        total = own(piece, 0, 0) + come[0].astype(jnp.float32) + come[1].astype(jnp.float32)
        sums.append(total.astype(jnp.bfloat16))
    first = jnp.concatenate(sums, axis=1)
    first = first.reshape(inner, columns // outer // inner, width)
    blocks = lax.all_to_all(first, "inner", split_axis=0, concat_axis=0, tiled=True)
    return jnp.sum(blocks, axis=0, dtype=jnp.float32)


def solution(mesh):
    inner, outer, tensor = (mesh.shape[name] for name in ("inner", "outer", "tensor"))
    fine = Mesh(
        mesh.devices.reshape(inner, outer // 2, 2, tensor), ("inner", "y", "core", "x")
    )
    in_specs = (P(("inner", "y", "core"), "x"), P(("inner", "y", "core", "x"), None))
    out_specs = P(("inner", "y", "core"), "x")
    return jax.shard_map(
        on_device, mesh=fine, in_specs=in_specs, out_specs=out_specs, check_vma=False
    )
```

```python
import jax
import jax.numpy as jnp
from jax import lax
from jax.sharding import Mesh, PartitionSpec as P

LANES = 128
SWAP = [(0, 1), (1, 0)]


def in_owner_order(out_grad, far, near, outer):
    columns = out_grad.shape[1]
    rows = columns // (far * near * outer * 2)
    new = lax.broadcasted_iota(jnp.int32, (columns, columns), 1)
    old = lax.broadcasted_iota(jnp.int32, (columns, columns), 0)
    row, rest = new % rows, new // rows
    f, rest = rest % far, rest // far
    n, rest = rest % near, rest // near
    y, core = rest % outer, rest // outer
    source = (((f * near + n) * outer + y) * 2 + core) * rows + row
    one_hot = (source == old).astype(out_grad.dtype)
    moved = lax.dot_general(
        out_grad, one_hot, (((1,), (0,)), ((), ())), preferred_element_type=jnp.float32
    )
    return moved.astype(out_grad.dtype)


def on_device(activations, out_grad):
    far_z, near_z, outer = (lax.axis_size(name) for name in ("far", "near", "y"))
    core, me, near = (lax.axis_index(name) for name in ("core", "y", "near"))
    inner = far_z * near_z
    width = activations.shape[1]
    ordered = in_owner_order(out_grad, far_z, near_z, outer)
    columns = ordered.shape[1] // 2

    def half_of(owner):
        return lax.dynamic_slice_in_dim(
            ordered, owner * columns, columns, 1, allow_negative_indices=False
        )

    grads_other = lax.ppermute(half_of(1 - core), "core", SWAP)
    grads_other, sent = lax.optimization_barrier((grads_other, activations))
    activations_other = lax.ppermute(sent, "core", SWAP)
    grads = jnp.stack([half_of(core), grads_other])
    grads = lax.all_gather(grads, "x", axis=1, tiled=True)
    tokens = jnp.concatenate([activations, activations_other], axis=0)
    chunks = lax.dot_general(
        grads.reshape(tokens.shape[0], columns),
        tokens,
        (((0,), (0,)), ((), ())),
        preferred_element_type=jnp.float32,
    ).astype(jnp.bfloat16).reshape(outer, columns // outer, width)
    cut = -(-(width // LANES) // 2) * LANES

    pairings = (
        [s ^ 1 for s in range(outer)],
        [(((s + outer - 1) ^ 1) + 1) % outer for s in range(outer)],
    )
    swaps = [
        [(2 * s + c, 2 * pairings[(c + k) % 2][s] + c) for s in range(outer) for c in (0, 1)]
        for k in (0, 1)
    ]
    way = (1 - 2 * lax.rem(me, 2)) * (1 - 2 * core)

    spans = ((0, cut), (cut, width))

    def own(piece, swap, distance):
        low, high = spans[piece]
        owner = lax.rem(me + way * (distance if swap == 0 else -distance) + outer, outer)
        block = lax.dynamic_slice(
            chunks, (owner, 0, low), (1, chunks.shape[1], high - low), allow_negative_indices=False
        )
        return block[0].astype(jnp.float32)

    farthest = outer // 2
    order = [(farthest, 0, 0), (farthest, 1, 1)]
    for distance in range(farthest - 1, 0, -1):
        first_way = (farthest - 1 - distance) % 2
        order += [(distance, p, p ^ first_way ^ late) for late in (0, 1) for p in (0, 1)]
    arrived, before = {}, {}
    for distance, piece, swap in order:
        block = own(piece, swap, distance)
        source = (distance + 1, piece, 1 - swap)
        if source in arrived:
            come, before[piece] = lax.optimization_barrier((arrived[source], before[piece]))
            block = (block + come.astype(jnp.float32)).astype(jnp.bfloat16)
        else:
            block = block.astype(jnp.bfloat16)
            if piece in before:
                block, before[1 - piece] = lax.optimization_barrier((block, before[1 - piece]))
        before[piece] = block
        arrived[distance, piece, swap] = lax.ppermute(block, ("y", "core"), swaps[swap])
    z_pairings = (
        [i ^ 1 for i in range(inner)],
        [(((i + inner - 1) ^ 1) + 1) % inner for i in range(inner)],
    )
    z_swap = [(2 * i + c, 2 * z_pairings[c][i] + c) for i in range(inner) for c in (0, 1)]
    half = columns // outer // near_z
    sums = []
    for piece in (0, 1):
        come = (arrived[1, piece, 0], arrived[1, piece, 1])
        total = own(piece, 0, 0) + come[0].astype(jnp.float32) + come[1].astype(jnp.float32)
        total = total.astype(jnp.bfloat16)

        def rows_of(parity):
            return lax.dynamic_slice_in_dim(
                total, parity * half, half, 0, allow_negative_indices=False
            )

        theirs = lax.ppermute(rows_of(1 - near), ("far", "near", "core"), z_swap)
        mine = rows_of(near).astype(jnp.float32) + theirs.astype(jnp.float32)
        sums.append(mine.astype(jnp.bfloat16))
    first = jnp.concatenate(sums, axis=1)
    first = first.reshape(far_z, half // far_z, width)
    blocks = lax.all_to_all(first, "far", split_axis=0, concat_axis=0, tiled=True)
    return jnp.sum(blocks, axis=0, dtype=jnp.float32)


def solution(mesh):
    inner, outer, tensor = (mesh.shape[name] for name in ("inner", "outer", "tensor"))
    fine = Mesh(
        mesh.devices.reshape(inner // 2, 2, outer // 2, 2, tensor),
        ("far", "near", "y", "core", "x"),
    )
    groups = ("far", "near", "y", "core")
    in_specs = (P(groups, "x"), P(groups + ("x",), None))
    return jax.shard_map(
        on_device, mesh=fine, in_specs=in_specs, out_specs=P(groups, "x"), check_vma=False
    )
```
